32 devices in a mesh: groups: 2 (over x), seq: 16 (over z, y, core).
Axes of the slice: x: 2, y: 2, z: 4, core: 2. Of those that a mesh axis runs over, the one named last changes fastest.
Arguments:
- queries: bfloat16 [8192, 4096], P(('groups', 'seq')), parts along dimension 0, may hold values from -6 to 6
- key_rows: bfloat16 [8192, 2048], P(('groups', 'seq')), parts along dimension 0, may hold values from -6 to 6
- value_matrix: bfloat16 [8192, 2048], P(('groups', 'seq')), parts along dimension 0, may hold values from -6 to 6
Outputs:
- attended: bfloat16 [8192, 4096], P(('groups', 'seq')), parts along dimension 0
The draws below stay inside these ranges and needn't reach their ends.
There are 2 independent parts, one for each index of `groups`. The reference program is written for one: setup_inputs(seed, part) draws one part's arguments, and reference() takes and returns one part's arrays. A program takes and returns all parts, laid end to end along the dimension named above; each array names one. Nothing has to cross between parts.
All inputs are finite; a program needn't handle non-finite values.
Results may differ from the reference program's by a relative error of at most 0.0045.
Values may be sent and summed in bfloat16 or wider, within the bound.
A program may use at most 64 MiB of HBM per device.

```python
import jax
import jax.numpy as jnp
from jax import lax

QUERY_HEADS = 32
KEY_VALUE_HEADS = 16
HEAD_WIDTH = 128
WINDOW = 1024
TOK_DEV = 256
SEQUENCE_LENGTH = 4096
REACH = 4
N_SEQ = 16


def draw_queries(key, part):
    own_key = jax.random.fold_in(key, 1)
    complete_shape = (SEQUENCE_LENGTH, QUERY_HEADS * HEAD_WIDTH)
    values_base = jnp.clip(jax.random.normal(own_key, complete_shape, jnp.float32), -6.0, 6.0)
    return values_base.astype(jnp.bfloat16)


def draw_key_rows(key, part):
    own_key = jax.random.fold_in(key, 2)
    complete_shape = (SEQUENCE_LENGTH, KEY_VALUE_HEADS * HEAD_WIDTH)
    values_base = jnp.clip(jax.random.normal(own_key, complete_shape, jnp.float32), -6.0, 6.0)
    return values_base.astype(jnp.bfloat16)


def block_levels(key, extent, pieces, smallest, high):
    loudness, own = 1.0, jax.random.fold_in(key, 6)
    for dim, parts in pieces:
        heights = jnp.exp(jax.random.uniform(jax.random.fold_in(own, dim), (parts,), jnp.float32, smallest / len(pieces), high / len(pieces)))
        loudness = loudness * jnp.repeat(heights, extent[dim] // parts).reshape([-1 if axis == dim else 1 for axis in range(len(extent))])
    return loudness


def bell_draw(key, dims, width, reach, split=(), kind=jnp.bfloat16):
    entries = jax.random.normal(key, dims, jnp.float32) * width
    if len(split) > 0:
        entries = block_levels(key, dims, split, -0.22, 0.18) * entries
    return jnp.clip(entries, min=-reach, max=reach).astype(kind)


def setup_inputs(seed: int = 0, part: int = 0) -> dict:
    key_of = jax.random.split(jax.random.key(seed), 4)
    part_keys = jax.random.split(jax.random.fold_in(key_of[3], part), 4)
    queries = draw_queries(jax.random.fold_in(jax.random.fold_in(key_of[3], part), 71), part)
    key_rows = draw_key_rows(jax.random.fold_in(jax.random.fold_in(key_of[3], part), 71), part)
    value_matrix = bell_draw(part_keys[2], (SEQUENCE_LENGTH, KEY_VALUE_HEADS * HEAD_WIDTH), 1.0, 6.0, ((0, 16),))
    return {"queries": queries, "key_rows": key_rows, "value_matrix": value_matrix}


score_scale = 168.0 ** -0.5
masked_value = -1.0e30


def attend_window(query_block, key_win, value_win, query_pos, key_pos):
    query_groups = QUERY_HEADS // KEY_VALUE_HEADS
    length = query_block.shape[0]
    visible = (key_pos[None, :] <= query_pos[:, None]) & (key_pos[None, :] > query_pos[:, None] - WINDOW) & (key_pos[None, :] >= 0)

    def head_count_ratio(head_index, output):
        query_head = lax.dynamic_slice_in_dim(query_block, head_index * query_groups * HEAD_WIDTH, query_groups * HEAD_WIDTH, 1).reshape(length, query_groups, HEAD_WIDTH)
        key_head = lax.dynamic_slice_in_dim(key_win, head_index * HEAD_WIDTH, HEAD_WIDTH, 1)
        value_head = lax.dynamic_slice_in_dim(value_win, head_index * HEAD_WIDTH, HEAD_WIDTH, 1)
        raw_scores = jnp.einsum("tgd,kd->gtk", query_head.astype(jnp.float32), key_head.astype(jnp.float32)) * score_scale
        raw_scores = jnp.where(visible[None], raw_scores, masked_value)
        row_max = jnp.max(raw_scores, axis=2)
        weights_full = jnp.where(visible[None], jnp.exp(raw_scores - row_max[:, :, None]), 0.0)
        row_total = jnp.sum(weights_full, axis=2)
        weights = weights_full.astype(jnp.bfloat16)
        weighted = jnp.einsum("gtk,kd->tgd", weights.astype(jnp.float32), value_head.astype(jnp.float32))
        result = weighted / jnp.transpose(row_total)[:, :, None]
        result = result.reshape(length, query_groups * HEAD_WIDTH).astype(jnp.bfloat16)
        return lax.dynamic_update_slice_in_dim(output, result, head_index * query_groups * HEAD_WIDTH, 1)

    return lax.fori_loop(0, KEY_VALUE_HEADS, head_count_ratio, jnp.zeros(query_block.shape, jnp.bfloat16))


def reference(queries, key_rows, value_matrix):
    length = TOK_DEV
    padding = REACH * length
    span = (REACH + 1) * length
    key_pad = jnp.concatenate([jnp.zeros((padding, key_rows.shape[1]), key_rows.dtype), key_rows], axis=0)
    value_pad = jnp.concatenate([jnp.zeros((padding, value_matrix.shape[1]), value_matrix.dtype), value_matrix], axis=0)

    def one_block(block_index):
        start = (block_index * length).astype(jnp.int32)
        query_block = lax.dynamic_slice_in_dim(queries, start, length, 0)
        key_win = lax.dynamic_slice_in_dim(key_pad, start, span, 0)
        value_win = lax.dynamic_slice_in_dim(value_pad, start, span, 0)
        query_pos = start + jnp.arange(length, dtype=jnp.int32)
        key_pos = start - padding + jnp.arange(span, dtype=jnp.int32)
        return attend_window(query_block, key_win, value_win, query_pos, key_pos)

    blocks_out = lax.map(one_block, jnp.arange(N_SEQ, dtype=jnp.int32))
    return blocks_out.reshape(SEQUENCE_LENGTH, QUERY_HEADS * HEAD_WIDTH)
```

```python
import functools
import math

import jax
import jax.numpy as jnp
from jax import lax
from jax.experimental import pallas as pl
from jax.experimental.pallas import tpu as pltpu
from jax.sharding import PartitionSpec as P

QUERY_HEADS = 32
KEY_VALUE_HEADS = 16
HEAD_WIDTH = 128
WINDOW = 1024

GROUP = QUERY_HEADS // KEY_VALUE_HEADS
HALF = 128
AHEAD = 4
EXPONENT = 168.0 ** (-0.5) * math.log2(math.e)
HIDDEN = 1e30


def kernel(
    n_seq, q_hbm, k_hbm, v_hbm, o_hbm,
    q_buf, k_buf, v_buf, o_buf, send_sem, recv_sem, q_sem, out_sem,
):
    rows = q_hbm.shape[0]
    chunks = k_buf.shape[0]
    reach = k_buf.shape[1] // rows - 1

    me = lax.axis_index("seq")
    place = me % 4
    odd = me % 2
    upper = place // 2
    sibling = me + 1 - 2 * odd
    across = me + 2 - 4 * upper
    has_prev = me >= 4
    has_next = me < n_seq - 4

    sources = (k_hbm, v_hbm)
    buffers = (k_buf, v_buf)

    def own(i, c):
        return sources[i].at[:, pl.ds(pl.multiple_of(c * HEAD_WIDTH, HEAD_WIDTH), HEAD_WIDTH)]

    def slot(i, c, hop):
        return buffers[i].at[c, pl.ds((reach - hop) * rows, rows), :]

    def send(i, c, source, hop, way, target):
        return pltpu.make_async_remote_copy(
            src_ref=source,
            dst_ref=slot(i, c, hop),
            send_sem=send_sem.at[way, c, i],
            recv_sem=recv_sem.at[hop, c, i],
            device_id={"seq": target},
            device_id_type=pl.DeviceIdType.MESH,
        )

    def own_copy(i, c):
        return pltpu.make_async_copy(own(i, c), slot(i, c, 0), recv_sem.at[0, c, i])

    def arrived(c, hop):
        for i in range(2):
            send(i, c, slot(i, c, hop), hop, 0, sibling).wait_recv()

    def out_copy(c):
        columns = pl.ds(pl.multiple_of(c * GROUP * HEAD_WIDTH, HEAD_WIDTH), GROUP * HEAD_WIDTH)
        return pltpu.make_async_copy(o_buf.at[:, columns], o_hbm.at[:, columns], out_sem.at[c])

    def send_own(c):
        @pl.when(has_next)
        def _():
            for i in range(2):
                send(i, c, own(i, c), 4, 0, me + 4).start()

        @pl.when(upper == 0)
        def _():
            for i in range(2):
                send(i, c, own(i, c), 2, 1, across).start()

        @pl.when(odd == 0)
        def _():
            for i in range(2):
                send(i, c, own(i, c), 1, 2, sibling).start()

        for i in range(2):
            own_copy(i, c).start()

    def relay_four(c):
        @pl.when(has_prev)
        def _():
            arrived(c, 4)

            @pl.when(upper == 1)
            def _():
                for i in range(2):
                    send(i, c, slot(i, c, 4), 2, 1, across).start()

            @pl.when(odd == 1)
            def _():
                for i in range(2):
                    send(i, c, slot(i, c, 4), 3, 2, sibling).start()

    def relay_two(c):
        @pl.when(me >= 2)
        def _():
            arrived(c, 2)

            @pl.when(odd == 0)
            def _():
                for i in range(2):
                    send(i, c, slot(i, c, 2), 3, 3, sibling).start()

            @pl.when(odd == 1)
            def _():
                for i in range(2):
                    send(i, c, slot(i, c, 2), 1, 3, sibling).start()

    def sent(c):
        def done(way):
            for i in range(2):
                send(i, c, slot(i, c, 0), 1, way, sibling).wait_send()

        @pl.when(has_next)
        def _():
            done(0)

        @pl.when(has_prev | (upper == 0))
        def _():
            done(1)

        @pl.when(has_prev | (odd == 0))
        def _():
            done(2)

        @pl.when(me >= 2)
        def _():
            done(3)

    lower = [jnp.where(me >= hop, 0.0, -HIDDEN).astype(jnp.float32) for hop in range(reach + 1)]

    def attend(c):
        @pl.when(me >= 1)
        def _():
            arrived(c, 1)

        @pl.when(me >= 3)
        def _():
            arrived(c, 3)

        for i in range(2):
            own_copy(i, c).wait()

        tile = (GROUP * HALF, HALF)
        query = lax.broadcasted_iota(jnp.int32, tile, 0) % HALF
        key = lax.broadcasted_iota(jnp.int32, tile, 1)
        for half in range(rows // HALF):
            low, size = half * HALF, rows * reach + HALF
            pieces = size // HALF
            hops = [reach - (low + piece * HALF) // rows for piece in range(pieces)]
            q_parts = [
                q_buf[
                    pl.ds(low, HALF),
                    pl.ds(pl.multiple_of((c * GROUP + g) * HEAD_WIDTH, HEAD_WIDTH), HEAD_WIDTH),
                ]
                for g in range(GROUP)
            ]
            q_tile = jnp.concatenate(q_parts, axis=0)
            scores = lax.dot_general(
                q_tile,
                k_buf[c, pl.ds(low, size), :],
                (((1,), (1,)), ((), ())),
                preferred_element_type=jnp.float32,
            )
            parts = [scores[:, piece * HALF : (piece + 1) * HALF] for piece in range(pieces)]
            parts[0] = jnp.where(key > query, parts[0], -HIDDEN)
            parts[-1] = jnp.where(key <= query, parts[-1], -HIDDEN)
            top = None
            for hop in range(reach + 1):
                here = None
                for piece in range(pieces):
                    if hops[piece] == hop:
                        here = parts[piece] if here is None else jnp.maximum(here, parts[piece])
                if hop > 0:
                    here = here + lower[hop]
                top = here if top is None else jnp.maximum(top, here)
            row_max = jnp.max(top, axis=1, keepdims=True) * EXPONENT
            shift = [row_max - lower[hop] if hop > 0 else row_max for hop in range(reach + 1)]
            total, weights = None, []
            for piece in range(pieces):
                full = jnp.exp2(parts[piece] * EXPONENT - shift[hops[piece]])
                total = full if total is None else total + full
                weights.append(full.astype(jnp.bfloat16))
            row_total = jnp.sum(total, axis=1, keepdims=True)
            weighted = jnp.dot(
                jnp.concatenate(weights, axis=1),
                v_buf[c, pl.ds(low, size), :],
                preferred_element_type=jnp.float32,
            )
            result = (weighted / row_total).astype(jnp.bfloat16)
            for g in range(GROUP):
                o_buf[
                    pl.ds(low, HALF),
                    pl.ds(pl.multiple_of((c * GROUP + g) * HEAD_WIDTH, HEAD_WIDTH), HEAD_WIDTH),
                ] = result[g * HALF : (g + 1) * HALF]
        out_copy(c).start()

    barrier = pltpu.get_barrier_semaphore()

    def greet(device):
        pl.semaphore_signal(
            barrier, inc=1, device_id={"seq": device}, device_id_type=pl.DeviceIdType.MESH
        )

    greet(sibling)
    greet(across)

    @pl.when(has_next)
    def _():
        greet(me + 4)

    @pl.when(has_prev)
    def _():
        greet(me - 4)

    q_copy = pltpu.make_async_copy(q_hbm, q_buf, q_sem)
    q_copy.start()

    pl.semaphore_wait(barrier, 2 + jnp.where(has_next, 1, 0) + jnp.where(has_prev, 1, 0))

    for c in range(min(AHEAD, chunks)):
        send_own(c)

    for hop in range(1, reach + 1):
        @pl.when(me < hop)
        def _(hop=hop):
            def clear(c, carry):
                for i in range(2):
                    buffers[i][c, pl.ds((reach - hop) * rows, rows), :] = jnp.zeros(
                        (rows, HEAD_WIDTH), jnp.bfloat16
                    )
                return carry

            lax.fori_loop(0, chunks, clear, 0)

    q_copy.wait()

    def step(j, carry):
        @pl.when(j + AHEAD < chunks)
        def _():
            send_own(j + AHEAD)

        @pl.when(j < chunks)
        def _():
            relay_four(j)

        @pl.when(j >= 2)
        def _():
            attend(j - 2)

        @pl.when((j >= 1) & (j <= chunks))
        def _():
            relay_two(j - 1)

        return carry

    lax.fori_loop(0, chunks + 2, step, 0)

    def finish(c, carry):
        sent(c)
        out_copy(c).wait()
        return carry

    lax.fori_loop(0, chunks, finish, 0)


def per_device(n_seq, queries, key_rows, value_matrix):
    rows = queries.shape[0]
    reach = (WINDOW - 1) // rows + 1
    chunks = KEY_VALUE_HEADS
    window = (chunks, (reach + 1) * rows, HEAD_WIDTH)
    pairs = QUERY_HEADS * rows * (WINDOW + HALF)
    return pl.pallas_call(
        functools.partial(kernel, n_seq),
        out_shape=jax.ShapeDtypeStruct(queries.shape, jnp.bfloat16),
        in_specs=[pl.BlockSpec(memory_space=pl.ANY)] * 3,
        out_specs=pl.BlockSpec(memory_space=pl.ANY),
        scratch_shapes=[
            pltpu.VMEM(queries.shape, jnp.bfloat16),
            pltpu.VMEM(window, jnp.bfloat16),
            pltpu.VMEM(window, jnp.bfloat16),
            pltpu.VMEM(queries.shape, jnp.bfloat16),
            pltpu.SemaphoreType.DMA((4, chunks, 2)),
            pltpu.SemaphoreType.DMA((reach + 1, chunks, 2)),
            pltpu.SemaphoreType.DMA,
            pltpu.SemaphoreType.DMA((chunks,)),
        ],
        compiler_params=pltpu.CompilerParams(
            collective_id=0, has_side_effects=True, vmem_limit_bytes=48 * 2**20
        ),
        cost_estimate=pl.CostEstimate(
            flops=4 * HEAD_WIDTH * pairs, bytes_accessed=16 * 2**20, transcendentals=pairs
        ),
    )(queries, key_rows, value_matrix)


def solution(mesh):
    spec = P(("groups", "seq"), None)
    return jax.shard_map(
        functools.partial(per_device, mesh.shape["seq"]),
        mesh=mesh,
        in_specs=(spec, spec, spec),
        out_specs=spec,
        check_vma=False,
    )
```

```python
import functools
import math

import jax
import jax.numpy as jnp
from jax import lax
from jax.experimental import pallas as pl
from jax.experimental.pallas import tpu as pltpu
from jax.sharding import PartitionSpec as P

QUERY_HEADS = 32
KEY_VALUE_HEADS = 16
HEAD_WIDTH = 128
WINDOW = 1024

GROUP = QUERY_HEADS // KEY_VALUE_HEADS
HALF = 128
AHEAD = 4
EXPONENT = 168.0 ** (-0.5) * math.log2(math.e)
HIDDEN = 1e30


def kernel(
    n_seq, q_hbm, k_hbm, v_hbm, o_hbm,
    q_buf, k_buf, v_buf, o_buf, send_sem, recv_sem, q_sem, out_sem,
):
    rows = q_hbm.shape[0]
    chunks = k_buf.shape[0]
    reach = k_buf.shape[1] // rows - 1

    me = lax.axis_index("seq")
    place = me % 4
    odd = me % 2
    upper = place // 2
    sibling = me + 1 - 2 * odd
    across = me + 2 - 4 * upper
    has_prev = me >= 4
    has_next = me < n_seq - 4

    sources = (k_hbm, v_hbm)
    buffers = (k_buf, v_buf)

    def own(i, c):
        return sources[i].at[:, pl.ds(pl.multiple_of(c * HEAD_WIDTH, HEAD_WIDTH), HEAD_WIDTH)]

    def slot(i, c, hop):
        return buffers[i].at[c, pl.ds((reach - hop) * rows, rows), :]

    def send(i, c, source, hop, way, target):
        return pltpu.make_async_remote_copy(
            src_ref=source,
            dst_ref=slot(i, c, hop),
            send_sem=send_sem.at[way, c, i],
            recv_sem=recv_sem.at[hop, c, i],
            device_id={"seq": target},
            device_id_type=pl.DeviceIdType.MESH,
        )

    def own_copy(i, c):
        return pltpu.make_async_copy(own(i, c), slot(i, c, 0), recv_sem.at[0, c, i])

    def arrived(i, c, hop):
        send(i, c, slot(i, c, hop), hop, 0, sibling).wait_recv()

    def out_copy(c):
        columns = pl.ds(pl.multiple_of(c * GROUP * HEAD_WIDTH, HEAD_WIDTH), GROUP * HEAD_WIDTH)
        return pltpu.make_async_copy(o_buf.at[:, columns], o_hbm.at[:, columns], out_sem.at[c])

    def send_own(c):
        @pl.when(has_next)
        def _():
            for i in range(2):
                send(i, c, own(i, c), 4, 0, me + 4).start()

        @pl.when(upper == 0)
        def _():
            for i in range(2):
                send(i, c, own(i, c), 2, 1, across).start()

        @pl.when(odd == 0)
        def _():
            for i in range(2):
                send(i, c, own(i, c), 1, 2, sibling).start()

        for i in range(2):
            own_copy(i, c).start()

    def relay_four(i, c):
        @pl.when(has_prev)
        def _():
            arrived(i, c, 4)

            @pl.when(upper == 1)
            def _():
                send(i, c, slot(i, c, 4), 2, 1, across).start()

            @pl.when(odd == 1)
            def _():
                send(i, c, slot(i, c, 4), 3, 2, sibling).start()

    def relay_two(i, c):
        @pl.when(me >= 2)
        def _():
            arrived(i, c, 2)

            @pl.when(odd == 0)
            def _():
                send(i, c, slot(i, c, 2), 3, 3, sibling).start()

            @pl.when(odd == 1)
            def _():
                send(i, c, slot(i, c, 2), 1, 3, sibling).start()

    def sent(c):
        def done(way):
            for i in range(2):
                send(i, c, slot(i, c, 0), 1, way, sibling).wait_send()

        @pl.when(has_next)
        def _():
            done(0)

        @pl.when(has_prev | (upper == 0))
        def _():
            done(1)

        @pl.when(has_prev | (odd == 0))
        def _():
            done(2)

        @pl.when(me >= 2)
        def _():
            done(3)

    lower = [jnp.where(me >= hop, 0.0, -HIDDEN).astype(jnp.float32) for hop in range(reach + 1)]

    def complete(i, c):
        @pl.when(me >= 1)
        def _():
            arrived(i, c, 1)

        @pl.when(me >= 3)
        def _():
            arrived(i, c, 3)

        own_copy(i, c).wait()

    def project(c, half, weights, row_total):
        low, size = half * HALF, rows * reach + HALF
        weighted = jnp.dot(
            weights, v_buf[c, pl.ds(low, size), :], preferred_element_type=jnp.float32
        )
        result = (weighted / row_total).astype(jnp.bfloat16)
        for g in range(GROUP):
            o_buf[
                pl.ds(low, HALF),
                pl.ds(pl.multiple_of((c * GROUP + g) * HEAD_WIDTH, HEAD_WIDTH), HEAD_WIDTH),
            ] = result[g * HALF : (g + 1) * HALF]

    def attend(c, last=False):
        complete(0, c)
        if not last:
            complete(1, c)

        halves = []
        tile = (GROUP * HALF, HALF)
        query = lax.broadcasted_iota(jnp.int32, tile, 0) % HALF
        key = lax.broadcasted_iota(jnp.int32, tile, 1)
        for half in range(rows // HALF):
            low, size = half * HALF, rows * reach + HALF
            pieces = size // HALF
            hops = [reach - (low + piece * HALF) // rows for piece in range(pieces)]
            q_parts = [
                q_buf[
                    pl.ds(low, HALF),
                    pl.ds(pl.multiple_of((c * GROUP + g) * HEAD_WIDTH, HEAD_WIDTH), HEAD_WIDTH),
                ]
                for g in range(GROUP)
            ]
            q_tile = jnp.concatenate(q_parts, axis=0)
            scores = lax.dot_general(
                q_tile,
                k_buf[c, pl.ds(low, size), :],
                (((1,), (1,)), ((), ())),
                preferred_element_type=jnp.float32,
            )
            parts = [scores[:, piece * HALF : (piece + 1) * HALF] for piece in range(pieces)]
            parts[0] = jnp.where(key > query, parts[0], -HIDDEN)
            parts[-1] = jnp.where(key <= query, parts[-1], -HIDDEN)
            top = None
            for hop in range(reach + 1):
                here = None
                for piece in range(pieces):
                    if hops[piece] == hop:
                        here = parts[piece] if here is None else jnp.maximum(here, parts[piece])
                if hop > 0:
                    here = here + lower[hop]
                top = here if top is None else jnp.maximum(top, here)
            row_max = jnp.max(top, axis=1, keepdims=True) * EXPONENT
            shift = [row_max - lower[hop] if hop > 0 else row_max for hop in range(reach + 1)]
            total, weights = None, []
            for piece in range(pieces):
                full = jnp.exp2(parts[piece] * EXPONENT - shift[hops[piece]])
                total = full if total is None else total + full
                weights.append(full.astype(jnp.bfloat16))
            halves.append(
                (jnp.concatenate(weights, axis=1), jnp.sum(total, axis=1, keepdims=True))
            )
            if not last:
                project(c, half, *halves[half])
        if last:
            complete(1, c)
            for half in range(rows // HALF):
                project(c, half, *halves[half])
        out_copy(c).start()

    barrier = pltpu.get_barrier_semaphore()

    def greet(device):
        pl.semaphore_signal(
            barrier, inc=1, device_id={"seq": device}, device_id_type=pl.DeviceIdType.MESH
        )

    greet(sibling)
    greet(across)

    @pl.when(has_next)
    def _():
        greet(me + 4)

    @pl.when(has_prev)
    def _():
        greet(me - 4)

    q_copy = pltpu.make_async_copy(q_hbm, q_buf, q_sem)
    q_copy.start()

    pl.semaphore_wait(barrier, 2 + jnp.where(has_next, 1, 0) + jnp.where(has_prev, 1, 0))

    for c in range(min(AHEAD, chunks)):
        send_own(c)

    for hop in range(1, reach + 1):
        @pl.when(me < hop)
        def _(hop=hop):
            def clear(c, carry):
                for i in range(2):
                    buffers[i][c, pl.ds((reach - hop) * rows, rows), :] = jnp.zeros(
                        (rows, HEAD_WIDTH), jnp.bfloat16
                    )
                return carry

            lax.fori_loop(0, chunks, clear, 0)

    q_copy.wait()

    def step(j, carry):
        @pl.when(j + AHEAD < chunks)
        def _():
            send_own(j + AHEAD)

        @pl.when(j >= 1)
        def _():
            relay_two(0, j - 1)
            relay_two(1, j - 1)

        relay_four(0, j)
        relay_four(1, j)

        @pl.when(j == chunks - 1)
        def _():
            relay_two(0, chunks - 1)

        @pl.when(j >= 1)
        def _():
            attend(j - 1)

        return carry

    lax.fori_loop(0, chunks, step, 0)
    relay_two(1, chunks - 1)
    attend(chunks - 1, last=True)

    def finish(c, carry):
        sent(c)
        out_copy(c).wait()
        return carry

    lax.fori_loop(0, chunks, finish, 0)


def per_device(n_seq, queries, key_rows, value_matrix):
    rows = queries.shape[0]
    reach = (WINDOW - 1) // rows + 1
    chunks = KEY_VALUE_HEADS
    window = (chunks, (reach + 1) * rows, HEAD_WIDTH)
    pairs = QUERY_HEADS * rows * (WINDOW + HALF)
    return pl.pallas_call(
        functools.partial(kernel, n_seq),
        out_shape=jax.ShapeDtypeStruct(queries.shape, jnp.bfloat16),
        in_specs=[pl.BlockSpec(memory_space=pltpu.HBM)] * 3,
        out_specs=pl.BlockSpec(memory_space=pl.ANY),
        scratch_shapes=[
            pltpu.VMEM(queries.shape, jnp.bfloat16),
            pltpu.VMEM(window, jnp.bfloat16),
            pltpu.VMEM(window, jnp.bfloat16),
            pltpu.VMEM(queries.shape, jnp.bfloat16),
            pltpu.SemaphoreType.DMA((4, chunks, 2)),
            pltpu.SemaphoreType.DMA((reach + 1, chunks, 2)),
            pltpu.SemaphoreType.DMA,
            pltpu.SemaphoreType.DMA((chunks,)),
        ],
        compiler_params=pltpu.CompilerParams(
            collective_id=0, has_side_effects=True, vmem_limit_bytes=48 * 2**20
        ),
        cost_estimate=pl.CostEstimate(
            flops=4 * HEAD_WIDTH * pairs, bytes_accessed=16 * 2**20, transcendentals=pairs
        ),
    )(queries, key_rows, value_matrix)


def solution(mesh):
    spec = P(("groups", "seq"), None)
    return jax.shard_map(
        functools.partial(per_device, mesh.shape["seq"]),
        mesh=mesh,
        in_specs=(spec, spec, spec),
        out_specs=spec,
        check_vma=False,
    )
```

```python
import functools
import math

import jax
import jax.numpy as jnp
from jax import lax
from jax.experimental import pallas as pl
from jax.experimental.pallas import tpu as pltpu
from jax.sharding import PartitionSpec as P

QUERY_HEADS = 32
KEY_VALUE_HEADS = 16
HEAD_WIDTH = 128
WINDOW = 1024

GROUP = QUERY_HEADS // KEY_VALUE_HEADS
HALF = 128
AHEAD = 4
EXPONENT = 168.0 ** (-0.5) * math.log2(math.e)
HIDDEN = 1e30


def kernel(
    n_seq, q_hbm, k_hbm, v_hbm, o_buf,
    q_buf, k_buf, v_buf, send_sem, recv_sem, q_sem,
):
    rows = q_hbm.shape[0]
    chunks = k_buf.shape[0]
    reach = k_buf.shape[1] // rows - 1

    me = lax.axis_index("seq")
    place = me % 4
    odd = me % 2
    upper = place // 2
    sibling = me + 1 - 2 * odd
    across = me + 2 - 4 * upper
    has_prev = me >= 4
    has_next = me < n_seq - 4

    sources = (k_hbm, v_hbm)
    buffers = (k_buf, v_buf)

    def own(i, c):
        return sources[i].at[:, pl.ds(pl.multiple_of(c * HEAD_WIDTH, HEAD_WIDTH), HEAD_WIDTH)]

    def slot(i, c, hop):
        return buffers[i].at[c, pl.ds((reach - hop) * rows, rows), :]

    def send(i, c, source, hop, way, target):
        return pltpu.make_async_remote_copy(
            src_ref=source,
            dst_ref=slot(i, c, hop),
            send_sem=send_sem.at[way, c, i],
            recv_sem=recv_sem.at[hop, c, i],
            device_id={"seq": target},
            device_id_type=pl.DeviceIdType.MESH,
        )

    def own_copy(i, c):
        return pltpu.make_async_copy(own(i, c), slot(i, c, 0), recv_sem.at[0, c, i])

    def arrived(i, c, hop):
        send(i, c, slot(i, c, hop), hop, 0, sibling).wait_recv()

    def send_own(c):
        @pl.when(has_next)
        def _():
            for i in range(2):
                send(i, c, own(i, c), 4, 0, me + 4).start()

        @pl.when(upper == 0)
        def _():
            for i in range(2):
                send(i, c, own(i, c), 2, 1, across).start()

        @pl.when(odd == 0)
        def _():
            for i in range(2):
                send(i, c, own(i, c), 1, 2, sibling).start()

        for i in range(2):
            own_copy(i, c).start()

    def relay_four(i, c):
        @pl.when(has_prev)
        def _():
            arrived(i, c, 4)

            @pl.when(upper == 1)
            def _():
                send(i, c, slot(i, c, 4), 2, 1, across).start()

            @pl.when(odd == 1)
            def _():
                send(i, c, slot(i, c, 4), 3, 2, sibling).start()

    def relay_two(i, c):
        @pl.when(me >= 2)
        def _():
            arrived(i, c, 2)

            @pl.when(odd == 0)
            def _():
                send(i, c, slot(i, c, 2), 3, 3, sibling).start()

            @pl.when(odd == 1)
            def _():
                send(i, c, slot(i, c, 2), 1, 3, sibling).start()

    def sent(c):
        def done(way):
            for i in range(2):
                send(i, c, slot(i, c, 0), 1, way, sibling).wait_send()

        @pl.when(has_next)
        def _():
            done(0)

        @pl.when(has_prev | (upper == 0))
        def _():
            done(1)

        @pl.when(has_prev | (odd == 0))
        def _():
            done(2)

        @pl.when(me >= 2)
        def _():
            done(3)

    lower = [jnp.where(me >= hop, 0.0, -HIDDEN).astype(jnp.float32) for hop in range(reach + 1)]

    def complete(i, c):
        @pl.when(me >= 1)
        def _():
            arrived(i, c, 1)

        @pl.when(me >= 3)
        def _():
            arrived(i, c, 3)

        own_copy(i, c).wait()

    def project(c, half, weights, row_total):
        low, size = half * HALF, rows * reach + HALF
        weighted = jnp.dot(
            weights, v_buf[c, pl.ds(low, size), :], preferred_element_type=jnp.float32
        )
        result = (weighted / row_total).astype(jnp.bfloat16)
        for g in range(GROUP):
            o_buf[
                pl.ds(low, HALF),
                pl.ds(pl.multiple_of((c * GROUP + g) * HEAD_WIDTH, HEAD_WIDTH), HEAD_WIDTH),
            ] = result[g * HALF : (g + 1) * HALF]

    def attend(c, last=False):
        complete(0, c)
        if not last:
            complete(1, c)

        halves = []
        tile = (GROUP * HALF, HALF)
        query = lax.broadcasted_iota(jnp.int32, tile, 0) % HALF
        key = lax.broadcasted_iota(jnp.int32, tile, 1)
        for half in range(rows // HALF):
            low, size = half * HALF, rows * reach + HALF
            pieces = size // HALF
            hops = [reach - (low + piece * HALF) // rows for piece in range(pieces)]
            q_parts = [
                q_buf[
                    pl.ds(low, HALF),
                    pl.ds(pl.multiple_of((c * GROUP + g) * HEAD_WIDTH, HEAD_WIDTH), HEAD_WIDTH),
                ]
                for g in range(GROUP)
            ]
            q_tile = jnp.concatenate(q_parts, axis=0)
            scores = lax.dot_general(
                q_tile,
                k_buf[c, pl.ds(low, size), :],
                (((1,), (1,)), ((), ())),
                preferred_element_type=jnp.float32,
            )
            parts = [scores[:, piece * HALF : (piece + 1) * HALF] for piece in range(pieces)]
            parts[0] = jnp.where(key > query, parts[0], -HIDDEN)
            parts[-1] = jnp.where(key <= query, parts[-1], -HIDDEN)
            top = None
            for hop in range(reach + 1):
                here = None
                for piece in range(pieces):
                    if hops[piece] == hop:
                        here = parts[piece] if here is None else jnp.maximum(here, parts[piece])
                if hop > 0:
                    here = here + lower[hop]
                top = here if top is None else jnp.maximum(top, here)
            row_max = jnp.max(top, axis=1, keepdims=True) * EXPONENT
            shift = [row_max - lower[hop] if hop > 0 else row_max for hop in range(reach + 1)]
            total, weights = None, []
            for piece in range(pieces):
                full = jnp.exp2(parts[piece] * EXPONENT - shift[hops[piece]])
                total = full if total is None else total + full
                weights.append(full.astype(jnp.bfloat16))
            halves.append(
                (jnp.concatenate(weights, axis=1), jnp.sum(total, axis=1, keepdims=True))
            )
            if not last:
                project(c, half, *halves[half])
        if last:
            complete(1, c)
            for half in range(rows // HALF):
                project(c, half, *halves[half])

    barrier = pltpu.get_barrier_semaphore()

    def greet(device):
        pl.semaphore_signal(
            barrier, inc=1, device_id={"seq": device}, device_id_type=pl.DeviceIdType.MESH
        )

    greet(sibling)
    greet(across)

    @pl.when(has_next)
    def _():
        greet(me + 4)

    @pl.when(has_prev)
    def _():
        greet(me - 4)

    q_copy = pltpu.make_async_copy(q_hbm, q_buf, q_sem)
    q_copy.start()

    pl.semaphore_wait(barrier, 2 + jnp.where(has_next, 1, 0) + jnp.where(has_prev, 1, 0))

    for c in range(min(AHEAD, chunks)):
        send_own(c)

    for hop in range(1, reach + 1):
        @pl.when(me < hop)
        def _(hop=hop):
            def clear(c, carry):
                for i in range(2):
                    buffers[i][c, pl.ds((reach - hop) * rows, rows), :] = jnp.zeros(
                        (rows, HEAD_WIDTH), jnp.bfloat16
                    )
                return carry

            lax.fori_loop(0, chunks, clear, 0)

    q_copy.wait()

    def step(j, carry):
        @pl.when(j + AHEAD < chunks)
        def _():
            send_own(j + AHEAD)

        @pl.when(j >= 1)
        def _():
            relay_two(0, j - 1)
            relay_two(1, j - 1)

        relay_four(0, j)
        relay_four(1, j)

        @pl.when(j == chunks - 1)
        def _():
            relay_two(0, chunks - 1)

        @pl.when(j >= 1)
        def _():
            attend(j - 1)

        return carry

    lax.fori_loop(0, chunks, step, 0)
    relay_two(1, chunks - 1)
    attend(chunks - 1, last=True)

    def finish(c, carry):
        sent(c)
        return carry

    lax.fori_loop(0, chunks, finish, 0)


def per_device(n_seq, queries, key_rows, value_matrix):
    rows = queries.shape[0]
    reach = (WINDOW - 1) // rows + 1
    chunks = KEY_VALUE_HEADS
    window = (chunks, (reach + 1) * rows, HEAD_WIDTH)
    pairs = QUERY_HEADS * rows * (WINDOW + HALF)
    return pl.pallas_call(
        functools.partial(kernel, n_seq),
        out_shape=pltpu.VMEM(queries.shape, jnp.bfloat16),
        in_specs=[pl.BlockSpec(memory_space=pltpu.HBM)] * 3,
        out_specs=pl.BlockSpec(memory_space=pltpu.VMEM),
        scratch_shapes=[
            pltpu.VMEM(queries.shape, jnp.bfloat16),
            pltpu.VMEM(window, jnp.bfloat16),
            pltpu.VMEM(window, jnp.bfloat16),
            pltpu.SemaphoreType.DMA((4, chunks, 2)),
            pltpu.SemaphoreType.DMA((reach + 1, chunks, 2)),
            pltpu.SemaphoreType.DMA,
        ],
        compiler_params=pltpu.CompilerParams(
            collective_id=0, has_side_effects=True, vmem_limit_bytes=56 * 2**20
        ),
        cost_estimate=pl.CostEstimate(
            flops=4 * HEAD_WIDTH * pairs, bytes_accessed=16 * 2**20, transcendentals=pairs
        ),
    )(queries, key_rows, value_matrix)


def solution(mesh):
    spec = P(("groups", "seq"), None)
    return jax.shard_map(
        functools.partial(per_device, mesh.shape["seq"]),
        mesh=mesh,
        in_specs=(spec, spec, spec),
        out_specs=spec,
        check_vma=False,
    )
```

```python
import functools
import math

import jax
import jax.numpy as jnp
from jax import lax
from jax.experimental import pallas as pl
from jax.experimental.pallas import tpu as pltpu
from jax.sharding import PartitionSpec as P

QUERY_HEADS = 32
KEY_VALUE_HEADS = 16
HEAD_WIDTH = 128
WINDOW = 1024

GROUP = QUERY_HEADS // KEY_VALUE_HEADS
HALF = 128
LAG = 4
AHEAD = 4
EXPONENT = 168.0 ** (-0.5) * math.log2(math.e)
HIDDEN = 1e30


def kernel(
    n_seq, q_hbm, k_hbm, v_hbm, o_buf,
    q_buf, k_buf, v_buf, send_sem, recv_sem, q_sem, far_sem,
):
    rows = q_hbm.shape[0]
    chunks = k_buf.shape[0]
    reach = k_buf.shape[1] // rows - 1

    me = lax.axis_index("seq")
    place = me % 4
    odd = me % 2
    upper = place // 2
    sibling = me + 1 - 2 * odd
    across = me + 2 - 4 * upper
    diagonal = across + 1 - 2 * odd
    has_prev = me >= 4
    has_next = me < n_seq - 4

    sources = (k_hbm, v_hbm)
    buffers = (k_buf, v_buf)

    def own(i, c):
        return sources[i].at[:, pl.ds(pl.multiple_of(c * HEAD_WIDTH, HEAD_WIDTH), HEAD_WIDTH)]

    def slot(i, c, hop):
        return buffers[i].at[c, pl.ds((reach - hop) * rows, rows), :]

    def send(i, c, source, hop, way, target):
        return pltpu.make_async_remote_copy(
            src_ref=source,
            dst_ref=slot(i, c, hop),
            send_sem=send_sem.at[way, c, i],
            recv_sem=recv_sem.at[hop, c, i],
            device_id={"seq": target},
            device_id_type=pl.DeviceIdType.MESH,
        )

    def own_copy(i, c):
        return pltpu.make_async_copy(own(i, c), slot(i, c, 0), recv_sem.at[0, c, i])

    def arrived(i, c, hop):
        send(i, c, slot(i, c, hop), hop, 0, sibling).wait_recv()

    def send_own(c):
        @pl.when(has_next)
        def _():
            for i in range(2):
                send(i, c, own(i, c), 4, 0, me + 4).start()

        @pl.when(upper == 0)
        def _():
            for i in range(2):
                send(i, c, own(i, c), 2, 1, across).start()

        @pl.when(odd == 0)
        def _():
            for i in range(2):
                send(i, c, own(i, c), 1, 2, sibling).start()

        for i in range(2):
            own_copy(i, c).start()

    def relay_four(i, c):
        @pl.when(has_prev)
        def _():
            arrived(i, c, 4)

            @pl.when(upper == 1)
            def _():
                send(i, c, slot(i, c, 4), 2, 1, across).start()

            @pl.when(odd == 1)
            def _():
                send(i, c, slot(i, c, 4), 3, 2, sibling).start()

    def far_copy(hop):
        return pltpu.make_async_remote_copy(
            src_ref=slot(1, chunks - 1, 4),
            dst_ref=slot(1, chunks - 1, hop),
            send_sem=far_sem,
            recv_sem=recv_sem.at[hop, chunks - 1, 1],
            device_id={"seq": diagonal},
            device_id_type=pl.DeviceIdType.MESH,
        )

    def relay_far():
        @pl.when(has_prev & (upper == 1) & (odd == 0))
        def _():
            far_copy(3).start()

        @pl.when(has_prev & (upper == 1) & (odd == 1))
        def _():
            far_copy(1).start()

    def relay_two(i, c):
        @pl.when(me >= 2)
        def _():
            arrived(i, c, 2)

            @pl.when(odd == 0)
            def _():
                send(i, c, slot(i, c, 2), 3, 3, sibling).start()

            @pl.when(odd == 1)
            def _():
                send(i, c, slot(i, c, 2), 1, 3, sibling).start()

    def sent(c):
        def done(way):
            for i in range(2):
                send(i, c, slot(i, c, 0), 1, way, sibling).wait_send()

        @pl.when(has_next)
        def _():
            done(0)

        @pl.when(has_prev | (upper == 0))
        def _():
            done(1)

        @pl.when(has_prev | (odd == 0))
        def _():
            done(2)

        @pl.when(me >= 2)
        def _():
            send(0, c, slot(0, c, 0), 1, 3, sibling).wait_send()

        @pl.when((me >= 2) & ((upper == 1) | (c < chunks - 1)))
        def _():
            send(1, c, slot(1, c, 0), 1, 3, sibling).wait_send()

    lower = [jnp.where(me >= hop, 0.0, -HIDDEN).astype(jnp.float32) for hop in range(reach + 1)]

    def complete(i, c):
        @pl.when(me >= 1)
        def _():
            arrived(i, c, 1)

        @pl.when(me >= 3)
        def _():
            arrived(i, c, 3)

        own_copy(i, c).wait()

    def project(c, half, weights, row_total):
        low, size = half * HALF, rows * reach + HALF
        weighted = jnp.dot(
            weights, v_buf[c, pl.ds(low, size), :], preferred_element_type=jnp.float32
        )
        result = (weighted / row_total).astype(jnp.bfloat16)
        for g in range(GROUP):
            o_buf[
                pl.ds(low, HALF),
                pl.ds(pl.multiple_of((c * GROUP + g) * HEAD_WIDTH, HEAD_WIDTH), HEAD_WIDTH),
            ] = result[g * HALF : (g + 1) * HALF]

    def attend(c, last=False):
        complete(0, c)
        if not last:
            complete(1, c)

        halves = []
        tile = (GROUP * HALF, HALF)
        query = lax.broadcasted_iota(jnp.int32, tile, 0) % HALF
        key = lax.broadcasted_iota(jnp.int32, tile, 1)
        for half in range(rows // HALF):
            low, size = half * HALF, rows * reach + HALF
            pieces = size // HALF
            hops = [reach - (low + piece * HALF) // rows for piece in range(pieces)]
            q_parts = [
                q_buf[
                    pl.ds(low, HALF),
                    pl.ds(pl.multiple_of((c * GROUP + g) * HEAD_WIDTH, HEAD_WIDTH), HEAD_WIDTH),
                ]
                for g in range(GROUP)
            ]
            q_tile = jnp.concatenate(q_parts, axis=0)
            scores = lax.dot_general(
                q_tile,
                k_buf[c, pl.ds(low, size), :],
                (((1,), (1,)), ((), ())),
                preferred_element_type=jnp.float32,
            )
            parts = [scores[:, piece * HALF : (piece + 1) * HALF] for piece in range(pieces)]
            parts[0] = jnp.where(key > query, parts[0], -HIDDEN)
            parts[-1] = jnp.where(key <= query, parts[-1], -HIDDEN)
            top = None
            for hop in range(reach + 1):
                here = None
                for piece in range(pieces):
                    if hops[piece] == hop:
                        here = parts[piece] if here is None else jnp.maximum(here, parts[piece])
                if hop > 0:
                    here = here + lower[hop]
                top = here if top is None else jnp.maximum(top, here)
            row_max = jnp.max(top, axis=1, keepdims=True) * EXPONENT
            shift = [row_max - lower[hop] if hop > 0 else row_max for hop in range(reach + 1)]
            total, weights = None, []
            for piece in range(pieces):
                full = jnp.exp2(parts[piece] * EXPONENT - shift[hops[piece]])
                total = full if total is None else total + full
                weights.append(full.astype(jnp.bfloat16))
            halves.append(
                (jnp.concatenate(weights, axis=1), jnp.sum(total, axis=1, keepdims=True))
            )
            if not last:
                project(c, half, *halves[half])
        if last:
            complete(1, c)

            @pl.when(has_prev & (upper == 0))
            def _():
                arrived(1, c, 2)

            for half in range(rows // HALF):
                project(c, half, *halves[half])

    barrier = pltpu.get_barrier_semaphore()

    def greet(device):
        pl.semaphore_signal(
            barrier, inc=1, device_id={"seq": device}, device_id_type=pl.DeviceIdType.MESH
        )

    greet(sibling)
    greet(across)
    greet(diagonal)

    @pl.when(has_next)
    def _():
        greet(me + 4)

    @pl.when(has_prev)
    def _():
        greet(me - 4)

    q_copy = pltpu.make_async_copy(q_hbm, q_buf, q_sem)
    q_copy.start()

    pl.semaphore_wait(barrier, 3 + jnp.where(has_next, 1, 0) + jnp.where(has_prev, 1, 0))

    for c in range(min(AHEAD, chunks)):
        send_own(c)

    for hop in range(1, reach + 1):
        @pl.when(me < hop)
        def _(hop=hop):
            def clear(c, carry):
                for i in range(2):
                    buffers[i][c, pl.ds((reach - hop) * rows, rows), :] = jnp.zeros(
                        (rows, HEAD_WIDTH), jnp.bfloat16
                    )
                return carry

            lax.fori_loop(0, chunks, clear, 0)

    q_copy.wait()

    def step(j, carry):
        @pl.when(j + AHEAD < chunks)
        def _():
            send_own(j + AHEAD)

        @pl.when(j >= 1)
        def _():
            relay_two(0, j - 1)
            relay_two(1, j - 1)

        relay_four(0, j)
        relay_four(1, j)

        @pl.when(j == chunks - 1)
        def _():
            relay_far()
            relay_two(0, chunks - 1)

        @pl.when(j >= 1)
        def _():
            attend(j - 1)

        @pl.when(j >= LAG)
        def _():
            sent(j - LAG)

        return carry

    lax.fori_loop(0, chunks, step, 0)

    @pl.when(upper == 1)
    def _():
        relay_two(1, chunks - 1)

    attend(chunks - 1, last=True)

    def finish(c, carry):
        sent(c)
        return carry

    lax.fori_loop(chunks - LAG, chunks, finish, 0)

    @pl.when(has_prev & (upper == 1))
    def _():
        far_copy(1).wait_send()


def per_device(n_seq, queries, key_rows, value_matrix):
    rows = queries.shape[0]
    reach = (WINDOW - 1) // rows + 1
    chunks = KEY_VALUE_HEADS
    window = (chunks, (reach + 1) * rows, HEAD_WIDTH)
    pairs = QUERY_HEADS * rows * (WINDOW + HALF)
    return pl.pallas_call(
        functools.partial(kernel, n_seq),
        out_shape=pltpu.VMEM(queries.shape, jnp.bfloat16),
        in_specs=[pl.BlockSpec(memory_space=pltpu.HBM)] * 3,
        out_specs=pl.BlockSpec(memory_space=pltpu.VMEM),
        scratch_shapes=[
            pltpu.VMEM(queries.shape, jnp.bfloat16),
            pltpu.VMEM(window, jnp.bfloat16),
            pltpu.VMEM(window, jnp.bfloat16),
            pltpu.SemaphoreType.DMA((4, chunks, 2)),
            pltpu.SemaphoreType.DMA((reach + 1, chunks, 2)),
            pltpu.SemaphoreType.DMA,
            pltpu.SemaphoreType.DMA,
        ],
        compiler_params=pltpu.CompilerParams(
            collective_id=0, has_side_effects=True, vmem_limit_bytes=56 * 2**20
        ),
        cost_estimate=pl.CostEstimate(
            flops=4 * HEAD_WIDTH * pairs, bytes_accessed=16 * 2**20, transcendentals=pairs
        ),
    )(queries, key_rows, value_matrix)


def solution(mesh):
    spec = P(("groups", "seq"), None)
    return jax.shard_map(
        functools.partial(per_device, mesh.shape["seq"]),
        mesh=mesh,
        in_specs=(spec, spec, spec),
        out_specs=spec,
        check_vma=False,
    )
```
